512 devices in a mesh: seq: 64 (over z, x, y_lo), tp: 8 (over y_hi, core).
Axes of the slice: x: 4, y: 8 (y_hi: 4, y_lo: 2; y = y_hi * 2 + y_lo), z: 8, core: 2. Of those that a mesh axis runs over, the one named last changes fastest.
Arguments:
- hidden_in: bfloat16 [8192, 5120], P('seq', 'tp'), may hold values from -6 to 6
- query_base: bfloat16 [8192, 5120], P('seq', 'tp'), may hold values from -10 to 10
- key_base: bfloat16 [8192, 5120], P('seq', 'tp'), may hold values from -10 to 10
- value_base: bfloat16 [8192, 5120], P('seq', 'tp'), may hold values from -6 to 6
- grad_out: bfloat16 [8192, 5120], P('seq', 'tp'), may hold values from -0.0625 to 0.0625
- adapter_down: bfloat16 [5120, 64], P('tp'), may hold values from -0.078125 to 0.078125
- adapter_up: bfloat16 [64, 5120], P(None, 'tp'), may hold values from -0.75 to 0.75
- tile_slot: int32 [8192], replicated, may hold values from 0 to 8191, as said below
- window_table: int32 [64, 4], P('seq'), may hold values from 0 to 63, as said below
Outputs:
- attended: bfloat16 [8192, 5120], P('seq', 'tp')
- grad_down: float32 [5120, 64], P('tp')
- grad_up: float32 [64, 5120], P(None, 'tp')
The draws below stay inside these ranges and needn't reach their ends.
Inputs may be any that keep to these rules, and one draw needn't show every extreme that they name: `tile_slot`: A permutation of the 8192 positions. The 128 tokens of each aligned block of 128 rows send exactly 2 tokens into each tile. `window_table`: row p lists p first, then 4 - 1 distinct tiles of the form (p + d) mod 64 with d nonzero and between -2 and 2, chosen and ordered per row.
All inputs are finite; a program needn't handle non-finite values.
Results may differ from the reference program's by a relative error of at most 0.012.
Values may be sent and summed in bfloat16 or wider, within the bound.
No kernel may reach another device: no remote copies, remote signals or barrier semaphores. Data moves between devices by JAX's collectives and lax.ppermute only.
A program may use at most 64 MiB of HBM per device.

```python
import math
import jax
import jax.numpy as jnp
from jax import lax

HEADS = 40
HEAD_DIM = 128
D = 5120
RANK = 64
TOK_DEV = 128
REACH = 2
WIN = 4
TILES = 64
TOKENS = 8192
PEER_ROWS = 2


def slot_table(key):
    key_source, key_target = jax.random.split(jax.random.fold_in(key, 11))
    local_order = jax.vmap(lambda subkey: jax.random.permutation(subkey, TOK_DEV))(jax.random.split(key_source, TILES))
    target = local_order // PEER_ROWS
    within = local_order % PEER_ROWS
    arrival = jax.vmap(lambda subkey: jax.random.permutation(subkey, TOK_DEV))(jax.random.split(key_target, TILES))
    source_ids = jnp.arange(TILES, dtype=jnp.int32)[:, None]
    flat_index = source_ids * PEER_ROWS + within
    slot_index = arrival[target, flat_index]
    return (target * TOK_DEV + slot_index).reshape(-1).astype(jnp.int32)


def draw_tile_slot(key, part):
    return slot_table(key)


def draw_window_table(key, part):
    key = jax.random.fold_in(key, 5)
    tile_ids = jnp.arange(TILES, dtype=jnp.int32)[:, None]
    offset_list = jnp.concatenate([jnp.arange(-REACH, 0, dtype=jnp.int32), jnp.arange(1, REACH + 1, dtype=jnp.int32)])
    columns = jnp.arange(2 * REACH, dtype=jnp.int32)[None, :]
    scores = jax.random.randint(key, (TILES, 2 * REACH), 0, 1000) * (2 * REACH) + columns
    picked = jnp.argsort(scores, axis=1)[:, :WIN - 1]
    chosen = (tile_ids + offset_list[picked]) % TILES
    return jnp.concatenate([tile_ids, chosen], axis=1).astype(jnp.int32)


def draw_query_base(key, part):
    key = jax.random.fold_in(key, 7)
    values_out = jnp.clip(jax.random.normal(key, (TOKENS, D), jnp.float32), -5.0, 5.0)
    return values_out.astype(jnp.bfloat16)


def draw_key_base(key, part):
    key = jax.random.fold_in(key, 9)
    values_out = jnp.clip(jax.random.normal(key, (TOKENS, D), jnp.float32), -5.0, 5.0)
    return values_out.astype(jnp.bfloat16)


def block_scale(stream_key, extent, cuts, smallest, top_value):
    def one(axis_at, shards_of):
        steps = jax.random.uniform(jax.random.fold_in(jax.random.fold_in(stream_key, 6), axis_at), (shards_of,), jnp.float32, smallest / len(cuts), top_value / len(cuts))
        return jnp.repeat(jnp.exp(steps), extent[axis_at] // shards_of).reshape((-1,) + (1,) * (len(extent) - axis_at - 1))

    factor_of = one(*cuts[0])
    for cut in cuts[1:]:
        factor_of = factor_of * one(*cut)
    return factor_of


def normal_values(key, extent, scale, most, cuts=(), held_as=jnp.bfloat16):
    loudness = block_scale(key, extent, cuts, -0.22, 0.18) if cuts else 1.0
    values = jax.random.normal(key, extent, jnp.float32) * scale * loudness
    return jnp.minimum(jnp.maximum(values, -most), most).astype(held_as)


def setup_inputs(seed: int = 0) -> dict:
    arg_keys = jax.random.split(jax.random.key(seed), 10)
    return {
        "hidden_in": normal_values(arg_keys[0], (TOKENS, D), 1.0, 6.0, ((0, 64), (1, 8))),
        "query_base": draw_query_base(jax.random.fold_in(arg_keys[9], 71), 0),
        "key_base": draw_key_base(jax.random.fold_in(arg_keys[9], 71), 0),
        "value_base": normal_values(arg_keys[3], (TOKENS, D), 1.0, 6.0, ((0, 64), (1, 8))),
        "grad_out": normal_values(arg_keys[4], (TOKENS, D), (TOKENS ** -0.5), 0.0625, ((0, 64), (1, 8))),
        "adapter_down": normal_values(arg_keys[5], (D, RANK), D ** -0.5, 0.078125, ((0, 8),)),
        "adapter_up": normal_values(arg_keys[6], (RANK, D), RANK ** -0.5, 0.75, ((1, 8),)),
        "tile_slot": draw_tile_slot(jax.random.fold_in(arg_keys[9], 71), 0),
        "window_table": draw_window_table(jax.random.fold_in(arg_keys[9], 71), 0),
    }


def attend(query, keys, values, grad_tile):
    scale = 1.0 / math.sqrt(HEAD_DIM)
    scores = jnp.einsum('qhd,khd->hqk', query.astype(jnp.float32), keys.astype(jnp.float32)) * scale
    weights = jax.nn.softmax(scores, axis=-1)
    weights_low = lax.optimization_barrier(weights.astype(jnp.bfloat16))
    head_out = jnp.einsum('hqk,khd->qhd', weights_low.astype(jnp.float32), values.astype(jnp.float32)).astype(jnp.bfloat16)
    grad_weights = jnp.einsum('qhd,khd->hqk', grad_tile.astype(jnp.float32), values.astype(jnp.float32))
    row_dot = lax.optimization_barrier(jnp.sum(weights * grad_weights, axis=-1, keepdims=True))
    grad_scores = lax.optimization_barrier((weights * (grad_weights - row_dot)).astype(jnp.bfloat16))
    grad_query = (jnp.einsum('hqk,khd->qhd', grad_scores.astype(jnp.float32), keys.astype(jnp.float32)) * scale).astype(jnp.bfloat16)
    return (head_out, grad_query)

def reference(hidden_in, query_base, key_base, value_base, grad_out, adapter_down, adapter_up, tile_slot, window_table):
    low_rank = jnp.dot(hidden_in, adapter_down, preferred_element_type=jnp.float32).astype(jnp.bfloat16)
    query = (query_base.astype(jnp.float32) + jnp.dot(low_rank, adapter_up, preferred_element_type=jnp.float32)).astype(jnp.bfloat16)

    def regroup(source_array):
        return jnp.zeros_like(source_array).at[tile_slot].set(source_array).reshape(TILES, TOK_DEV, HEADS, HEAD_DIM)
    query_tile = regroup(query)
    key_tile = regroup(key_base)
    value_tile = regroup(value_base)
    grad_tile = regroup(grad_out)

    def tile_work(tile_index):
        chosen = window_table[tile_index]
        keys = key_tile[chosen].reshape(WIN * TOK_DEV, HEADS, HEAD_DIM)
        values = value_tile[chosen].reshape(WIN * TOK_DEV, HEADS, HEAD_DIM)
        return attend(query_tile[tile_index], keys, values, grad_tile[tile_index])
    out_tile, grad_query_tile = lax.map(tile_work, jnp.arange(TILES, dtype=jnp.int32))
    attended = out_tile.reshape(TOKENS, D)[tile_slot]
    grad_query = grad_query_tile.reshape(TOKENS, D)[tile_slot]
    grad_up = jnp.dot(low_rank.T, grad_query, preferred_element_type=jnp.float32)
    low_grad = jnp.dot(grad_query, adapter_up.T, preferred_element_type=jnp.float32).astype(jnp.bfloat16)
    grad_down = jnp.dot(hidden_in.T, low_grad, preferred_element_type=jnp.float32)
    return (attended, grad_down, grad_up)
```

```python
import functools
import math

import jax
import jax.numpy as jnp
from jax import lax
from jax.experimental import pallas as pl
from jax.experimental.pallas import tpu as pltpu
from jax.sharding import PartitionSpec as P

HEAD_DIM = 128
REACH = 2
VMEM_BYTES = 48 * 1024 * 1024
NT = (((1,), (1,)), ((), ()))
NN = (((1,), (0,)), ((), ()))
TN = (((0,), (0,)), ((), ()))


def product(left, right, dims=NN):
    return lax.dot_general(left, right, dims, preferred_element_type=jnp.float32)


def shifted(shard, by):
    devices = lax.axis_size("seq")
    return lax.ppermute(shard, "seq", [(i, (i + by) % devices) for i in range(devices)])


def swap(blocks, axis):
    return lax.all_to_all(blocks, axis, split_axis=0, concat_axis=0, tiled=True)


def call(body, out_shape, prefetch=(), operands=(), in_specs=None, cost=None):
    def whole(shape):
        return pl.BlockSpec(shape, lambda i, *_: (0,) * len(shape))

    outs = out_shape if isinstance(out_shape, (list, tuple)) else [out_shape]
    specs = in_specs or [None] * len(operands)
    return pl.pallas_call(
        body,
        out_shape=out_shape,
        grid_spec=pltpu.PrefetchScalarGridSpec(
            num_scalar_prefetch=len(prefetch),
            grid=(1,),
            in_specs=[s or whole(o.shape) for s, o in zip(specs, operands)],
            out_specs=jax.tree.map(lambda o: whole(o.shape), out_shape),
        ),
        compiler_params=pltpu.CompilerParams(vmem_limit_bytes=VMEM_BYTES),
        cost_estimate=cost,
    )(*prefetch, *operands)


def low_rank_kernel(hidden, down_t, parts):
    part = product(down_t[...], hidden[...], NT)
    for k in range(parts.shape[0]):
        parts[k] = part


def order_kernel(me, slots, key, value, order, send):
    tokens = order.shape[0]
    target = slots[0] // tokens
    rows = lax.broadcasted_iota(jnp.int32, (tokens, tokens), 0)
    cols = lax.broadcasted_iota(jnp.int32, (tokens, tokens), 1)
    spread = jnp.broadcast_to(target, (tokens, tokens))
    target_col = jnp.sum(jnp.where(rows == cols, spread, 0), axis=1, keepdims=True)
    earlier = jnp.logical_and(target_col == spread, rows < cols)
    rank = jnp.sum(jnp.where(earlier, 1, 0), axis=0, keepdims=True)
    place = target * (tokens // lax.axis_size("seq")) + rank
    one_hot = jnp.where(rows == place, 1.0, 0.0).astype(jnp.bfloat16)
    order[...] = one_hot
    width = key.shape[1]
    send[:, :width] = product(one_hot, key[...]).astype(jnp.bfloat16)
    send[:, width:] = product(one_hot, value[...]).astype(jnp.bfloat16)


def query_kernel(parts, query_base, grad, hidden, up, order, send):
    tokens, width = query_base.shape
    rank = up.shape[0]
    total = parts[0]
    for k in range(1, parts.shape[0]):
        total = total + parts[k]
    low_t = total.astype(jnp.bfloat16)
    query = (query_base[...].astype(jnp.float32) + product(low_t, up[...], TN)).astype(jnp.bfloat16)
    one_hot = order[...]
    send[:, :width] = product(one_hot, query).astype(jnp.bfloat16)
    send[:, width : 2 * width] = product(one_hot, grad[...]).astype(jnp.bfloat16)
    send[:, 2 * width : 3 * width] = product(one_hot, hidden[...]).astype(jnp.bfloat16)
    send[:, 3 * width : 3 * width + rank] = product(one_hot, low_t, NT).astype(jnp.bfloat16)
    send[:, 3 * width + rank :] = jnp.zeros((tokens, send.shape[1] - 3 * width - rank), jnp.bfloat16)


def attend_kernel(tiles, me, window, kv_own, kv_a, kv_b, kv_c, kv_d, rows, up, out, low_parts, up_part):
    tokens = kv_own.shape[0]
    width = out.shape[1]
    rank = up.shape[0]
    missing = jnp.int32(6)
    for k in range(1, 4):
        away = lax.rem(window[k] - me[0] + tiles, tiles)
        missing = missing - jnp.where(away <= REACH, away + 1, away - (tiles - REACH))
    near = (kv_own, kv_a, kv_b, kv_c, kv_d)

    scale = 1.0 / math.sqrt(HEAD_DIM)
    low = rows[:, 3 * width : 3 * width + rank]
    low_total = jnp.zeros((rank, tokens), jnp.float32)
    for h in range(width // HEAD_DIM):
        columns = slice(h * HEAD_DIM, (h + 1) * HEAD_DIM)
        value_columns = slice(width + h * HEAD_DIM, width + (h + 1) * HEAD_DIM)
        keys = jnp.concatenate(
            [kv_own[:, columns]]
            + [jnp.where(missing < k, near[k + 1][:, columns], near[k][:, columns]) for k in (1, 2, 3)],
            axis=0,
        )
        values = jnp.concatenate(
            [kv_own[:, value_columns]]
            + [jnp.where(missing < k, near[k + 1][:, value_columns], near[k][:, value_columns]) for k in (1, 2, 3)],
            axis=0,
        )
        query = rows[:, columns]
        grad = rows[:, value_columns]
        scores = product(query, keys, NT) * scale
        exps = jnp.exp(scores - jnp.max(scores, axis=-1, keepdims=True))
        weights = exps / jnp.sum(exps, axis=-1, keepdims=True)
        out[:, columns] = product(weights.astype(jnp.bfloat16), values).astype(jnp.bfloat16)
        grad_weights = product(grad, values, NT)
        row_dot = jnp.sum(weights * grad_weights, axis=-1, keepdims=True)
        grad_scores = (weights * (grad_weights - row_dot)).astype(jnp.bfloat16)
        grad_query = (product(grad_scores, keys) * scale).astype(jnp.bfloat16)
        low_total = low_total + product(up[:, columns], grad_query, NT)
        up_part[:, columns] = product(low, grad_query, TN)
    for k in range(low_parts.shape[0]):
        low_parts[k] = low_total


def down_kernel(parts, hidden, down_part):
    total = parts[0]
    for k in range(1, parts.shape[0]):
        total = total + parts[k]
    down_part[...] = product(total.astype(jnp.bfloat16), hidden[...])


def restore_kernel(order, back, attended):
    attended[...] = product(order[...], back[...], TN).astype(jnp.bfloat16)


def local(
    hidden_in,
    query_base,
    key_base,
    value_base,
    grad_out,
    adapter_down,
    adapter_up,
    tile_slot,
    window_table,
):
    tokens, width = hidden_in.shape
    rank = adapter_up.shape[0]
    tiles = lax.axis_size("seq")
    group = lax.axis_size("tp")
    peer = tokens // tiles
    bf16, f32 = jnp.bfloat16, jnp.float32
    shape = jax.ShapeDtypeStruct
    me = lax.axis_index("seq").astype(jnp.int32).reshape(1)

    low_parts = swap(
        call(low_rank_kernel, shape((group, rank, tokens), f32), (), (hidden_in, adapter_down.T)), "tp"
    )
    order, kv_send = call(
        order_kernel,
        [shape((tokens, tokens), bf16), shape((tokens, 2 * width), bf16)],
        (me,),
        (tile_slot.reshape(tiles, 1, tokens), key_base, value_base),
        [pl.BlockSpec((1, 1, tokens), lambda i, me: (me[0], 0, 0)), None, None],
    )
    kv_own = swap(kv_send.reshape(tiles, peer, -1), "seq").reshape(tokens, -1)
    kv_near = [shifted(kv_own, by) for by in (2, 1, -1, -2)]
    row_send = call(
        query_kernel,
        shape((tokens, 3 * width + 128), bf16),
        (),
        (low_parts, query_base, grad_out, hidden_in, adapter_up, order),
    )
    rows = swap(row_send.reshape(tiles, peer, -1), "seq").reshape(tokens, -1)
    out_tile, low_grad_parts, up_part = call(
        functools.partial(attend_kernel, tiles),
        [shape((tokens, width), bf16), shape((group, rank, tokens), f32), shape((rank, width), f32)],
        (me, window_table[0]),
        (kv_own, *kv_near, rows, adapter_up),
    )
    low_grad_parts = swap(low_grad_parts, "tp")
    up_rows = swap(up_part.reshape(rank, 1, width), "seq")
    back = swap(out_tile.reshape(tiles, peer, width), "seq").reshape(tokens, width)
    down_part = call(
        down_kernel,
        shape((rank, width), f32),
        (),
        (low_grad_parts, rows),
        [None, pl.BlockSpec((tokens, width), lambda i: (0, 2))],
    )
    down_rows = swap(down_part.reshape(rank, 1, width), "seq")
    sums = jnp.concatenate([jnp.sum(up_rows, axis=0), jnp.sum(down_rows, axis=0)], axis=-1)
    totals = swap(jnp.broadcast_to(sums[None], (tiles, 1, 2 * width)), "seq").reshape(rank, 2 * width)
    attended = call(restore_kernel, shape((tokens, width), bf16), (), (order, back))
    return attended, totals[:, width:].T, totals[:, :width]


def solution(mesh):
    return jax.shard_map(
        local,
        mesh=mesh,
        in_specs=(
            P("seq", "tp"),
            P("seq", "tp"),
            P("seq", "tp"),
            P("seq", "tp"),
            P("seq", "tp"),
            P("tp", None),
            P(None, "tp"),
            P(),
            P("seq", None),
        ),
        out_specs=(P("seq", "tp"), P("tp", None), P(None, "tp")),
        check_vma=False,
    )
```

```python
import functools
import math

import jax
import jax.numpy as jnp
from jax import lax
from jax.experimental import pallas as pl
from jax.experimental.pallas import tpu as pltpu
from jax.sharding import Mesh
from jax.sharding import PartitionSpec as P

HEAD_DIM = 128
REACH = 2
VMEM_BYTES = 48 * 1024 * 1024
START_BYTES = 60 * 1024 * 1024
SEQ = ("pair", "lane")
HEADS_OF = ((0, 1, 2), (3, 4, 2))
UNITS = ((0, 0), (0, 1), (1, 0), (1, 1), (2, None))
NT = (((1,), (1,)), ((), ()))
NN = (((1,), (0,)), ((), ()))
TN = (((0,), (0,)), ((), ()))


def product(left, right, dims=NN):
    return lax.dot_general(left, right, dims, preferred_element_type=jnp.float32)


def shifted(shard, by):
    devices = lax.axis_size("pair")
    return lax.ppermute(shard, "pair", [(i, (i + by) % devices) for i in range(devices)])


def swap(blocks, axis):
    return lax.all_to_all(blocks, axis, split_axis=0, concat_axis=0, tiled=True)


def call(body, out_shape, prefetch=(), operands=(), in_specs=None, vmem=VMEM_BYTES):
    def whole(shape):
        return pl.BlockSpec(shape, lambda i, *_: (0,) * len(shape))

    specs = in_specs or [None] * len(operands)
    return pl.pallas_call(
        body,
        out_shape=out_shape,
        grid_spec=pltpu.PrefetchScalarGridSpec(
            num_scalar_prefetch=len(prefetch),
            grid=(1,),
            in_specs=[s or whole(o.shape) for s, o in zip(specs, operands)],
            out_specs=jax.tree.map(lambda o: whole(o.shape), out_shape),
        ),
        compiler_params=pltpu.CompilerParams(vmem_limit_bytes=vmem),
    )(*prefetch, *operands)


def head(array, index):
    return array[:, index * HEAD_DIM : (index + 1) * HEAD_DIM]


def start_kernel(me, slots, key, value, query_base, grad, hidden, down_t, order, send, part):
    tokens = order.shape[0]
    pairs, lanes, peer, _ = send.shape
    width = key.shape[1]
    part[...] = product(down_t[...], hidden[...], NT)
    target = slots[0] // tokens
    rows = lax.broadcasted_iota(jnp.int32, (tokens, tokens), 0)
    cols = lax.broadcasted_iota(jnp.int32, (tokens, tokens), 1)
    spread = jnp.broadcast_to(target, (tokens, tokens))
    target_col = jnp.sum(jnp.where(rows == cols, spread, 0), axis=1, keepdims=True)
    earlier = jnp.logical_and(target_col == spread, rows < cols)
    rank = jnp.sum(jnp.where(earlier, 1, 0), axis=0, keepdims=True)
    half = pairs * peer
    place = lax.rem(target, lanes) * half + lax.div(target, jnp.int32(lanes)) * peer + rank
    one_hot = jnp.where(rows == place, 1.0, 0.0).astype(jnp.bfloat16)
    order[...] = one_hot

    def by_tile(source):
        moved = product(one_hot, source[...]).astype(jnp.bfloat16)
        return [moved[k * half : (k + 1) * half] for k in range(lanes)]

    def put(lane, start, block):
        send[:, lane, :, start : start + block.shape[1]] = block.reshape(pairs, peer, block.shape[1])

    shared = len(HEADS_OF[0]) * HEAD_DIM
    for k, source in enumerate((key, value)):
        moved = by_tile(source)
        for lane in range(lanes):
            for tile in range(lanes):
                for j, h in enumerate(HEADS_OF[lane]):
                    put(lane, (2 * tile + k) * shared + j * HEAD_DIM, head(moved[tile], h))
    start = 2 * lanes * shared
    for source in (query_base, grad):
        moved = by_tile(source)
        for lane in range(lanes):
            for unit, (j, tile) in enumerate(UNITS):
                put(lane, start + unit * HEAD_DIM, head(moved[lane if tile is None else tile], HEADS_OF[lane][j]))
        start += width


def add_up(parts):
    total = parts[0].astype(jnp.float32)
    for k in range(1, parts.shape[0]):
        total = total + parts[k].astype(jnp.float32)
    return total.astype(jnp.bfloat16)


def second_kernel(parts, hidden, order, send):
    pairs, lanes, peer, _ = send.shape
    half = pairs * peer
    width = hidden.shape[1]
    one_hot = order[...]
    moved = product(one_hot, hidden[...]).astype(jnp.bfloat16)
    low = product(one_hot, add_up(parts), NT).astype(jnp.bfloat16)
    low = jnp.concatenate([low[k * half : (k + 1) * half] for k in range(lanes)], axis=1)
    for lane in range(lanes):
        send[:, lane, :, :width] = moved[lane * half : (lane + 1) * half].reshape(pairs, peer, width)
        send[:, lane, :, width:] = low.reshape(pairs, peer, low.shape[1])


def unpack_kernel(received, after, key_value):
    tokens, width = key_value.shape[0] // 2, key_value.shape[1]
    for tile in range(2):
        key_value[tile * tokens : (tile + 1) * tokens, :] = received[:, :, tile * width : (tile + 1) * width].reshape(
            tokens, width
        )


def query_kernel(first, second, up, lane, query, grad, hidden, low):
    tokens, width = query.shape
    rank = up.shape[0]
    start = first.shape[2] - 2 * width
    low[...] = second[:, :, width:].reshape(tokens, 2 * rank)
    own = lane[0] == 0
    ups = own_heads(up, own)
    low_own = jnp.where(own, low[:, :rank], low[:, rank:])
    for unit, (j, tile) in enumerate(UNITS):
        columns = slice(start + unit * HEAD_DIM, start + (unit + 1) * HEAD_DIM)
        base = first[:, :, columns].reshape(tokens, HEAD_DIM).astype(jnp.float32)
        rows = low_own if tile is None else low[:, tile * rank : (tile + 1) * rank]
        query[:, unit * HEAD_DIM : (unit + 1) * HEAD_DIM] = (base + product(rows, ups[j])).astype(jnp.bfloat16)
    grad[...] = first[:, :, start + width : start + 2 * width].reshape(tokens, width)
    hidden[...] = second[:, :, :width].reshape(tokens, width)


def own_heads(up, own):
    return [jnp.where(own, head(up, a), head(up, b)) for a, b in zip(*HEADS_OF)]


def attend_kernel(
    tiles, lane, window_a, window_b, left, right, centre, queries, grads, low, up, out, low_parts, up_part
):
    tokens = queries.shape[0]
    rank = up.shape[0]
    own = lane[0] == 0
    missing = []
    for tile in range(2):
        total = jnp.int32(0)
        mine = lane[0] == tile
        row = [jnp.where(mine, window_a[k], window_b[k]) for k in range(4)]
        for k in range(1, 4):
            away = lax.rem(row[k] - row[0] + tiles, tiles)
            total = total + jnp.where(away <= REACH, away + REACH, away - (tiles - REACH))
        missing.append(8 - total)
    span = [(array, tile) for array in (left, centre, right) for tile in range(2)]

    def block(index, columns):
        array, tile = span[index]
        return array[tile * tokens : (tile + 1) * tokens, columns]

    def chosen(tile, columns):
        if tile is None:
            skip = jnp.where(own, missing[0], missing[1])
            blocks = []
            for k in range(4):
                near = jnp.where(own, block(k, columns), block(k + 1, columns))
                far = jnp.where(own, block(k + 1, columns), block(k + 2, columns))
                blocks.append(jnp.where(skip <= k, far, near))
            return jnp.concatenate(blocks, axis=0)
        return jnp.concatenate(
            [
                jnp.where(missing[tile] <= k, block(tile + k + 1, columns), block(tile + k, columns))
                for k in range(4)
            ],
            axis=0,
        )

    scale = 1.0 / math.sqrt(HEAD_DIM)
    ups = own_heads(up, own)
    low_own = jnp.where(own, low[:, :rank], low[:, rank:])
    low_of = [jnp.zeros((rank, tokens), jnp.float32) for _ in range(2)]
    up_of = [jnp.zeros((rank, HEAD_DIM), jnp.float32) for _ in ups]
    shared = len(ups) * HEAD_DIM
    for unit, (j, tile) in enumerate(UNITS):
        columns = slice(unit * HEAD_DIM, (unit + 1) * HEAD_DIM)
        keys = chosen(tile, slice(j * HEAD_DIM, (j + 1) * HEAD_DIM))
        values = chosen(tile, slice(shared + j * HEAD_DIM, shared + (j + 1) * HEAD_DIM))
        scores = product(queries[:, columns], keys, NT) * scale
        exps = jnp.exp(scores - jnp.max(scores, axis=-1, keepdims=True))
        weights = exps * (1.0 / jnp.sum(exps, axis=-1, keepdims=True))
        out[:, columns] = product(weights.astype(jnp.bfloat16), values).astype(jnp.bfloat16)
        grad_weights = product(grads[:, columns], values, NT)
        row_dot = jnp.sum(weights * grad_weights, axis=-1, keepdims=True)
        grad_scores = (weights * (grad_weights - row_dot)).astype(jnp.bfloat16)
        grad_query = (product(grad_scores, keys) * scale).astype(jnp.bfloat16)
        low_grad = product(ups[j], grad_query, NT)
        rows = low_own if tile is None else low[:, tile * rank : (tile + 1) * rank]
        up_of[j] = up_of[j] + product(rows, grad_query, TN)
        if tile is None:
            low_of = [
                low_of[0] + jnp.where(own, low_grad, 0.0),
                low_of[1] + jnp.where(own, 0.0, low_grad),
            ]
        else:
            low_of[tile] = low_of[tile] + low_grad
    group = low_parts.shape[0] // 2
    for k in range(low_parts.shape[0]):
        low_parts[k] = low_of[k // group].astype(low_parts.dtype)
    for h in range(up_part.shape[1] // HEAD_DIM):
        halves = [up_of[heads.index(h)] if h in heads else jnp.zeros_like(up_of[0]) for heads in HEADS_OF]
        up_part[:, h * HEAD_DIM : (h + 1) * HEAD_DIM] = jnp.where(own, halves[0], halves[1])


def down_kernel(parts, hidden, out, up_part, send):
    tokens, width = out.shape
    peers, peer, _ = send.shape
    down_part = product(add_up(parts), hidden[...])
    sums = jnp.concatenate([up_part[...], down_part], axis=0).astype(jnp.bfloat16)
    send[:, :, :width] = out[...].reshape(peers, peer, width)
    send[:, :, width:] = sums.reshape(peers, peer, width)


def sum_kernel(received, totals):
    width = totals.shape[2]
    total = jnp.sum(received[:, :, width:].astype(jnp.float32), axis=0, keepdims=True)
    totals[...] = jnp.broadcast_to(total, totals.shape).astype(totals.dtype)


def restore_kernel(order, received, attended):
    tokens, width = attended.shape
    pairs, lanes, peer, _ = received.shape
    tiles = []
    for tile in range(lanes):
        blocks = []
        for h in range(width // HEAD_DIM):
            for lane, heads in enumerate(HEADS_OF):
                for unit, (j, at) in enumerate(UNITS):
                    if heads[j] == h and (lane if at is None else at) == tile:
                        columns = slice(unit * HEAD_DIM, (unit + 1) * HEAD_DIM)
                        blocks.append(received[:, lane, :, columns].reshape(pairs * peer, HEAD_DIM))
        tiles.append(jnp.concatenate(blocks, axis=1))
    attended[...] = product(order[...], jnp.concatenate(tiles, axis=0), TN).astype(jnp.bfloat16)


def split_kernel(totals, up_total, down_total):
    rank, width = up_total.shape
    rows = totals[...].reshape(2 * rank, width).astype(jnp.float32)
    up_total[...] = rows[:rank]
    down_total[...] = rows[rank:]


def local(
    hidden_in,
    query_base,
    key_base,
    value_base,
    grad_out,
    adapter_down,
    adapter_up,
    tile_slot,
    window_table,
):
    tokens, width = hidden_in.shape
    rank = adapter_up.shape[0]
    tiles = lax.axis_size(SEQ)
    lanes = lax.axis_size("lane")
    pairs = tiles // lanes
    group = lax.axis_size("tp")
    peer = tokens // tiles
    shared = len(HEADS_OF[0]) * HEAD_DIM
    bf16, f32 = jnp.bfloat16, jnp.float32
    shape = jax.ShapeDtypeStruct
    me = lax.axis_index(SEQ).astype(jnp.int32).reshape(1)
    lane = lax.axis_index("lane").astype(jnp.int32).reshape(1)
    window = window_table.reshape(-1)
    other_window = lax.ppermute(window, "lane", [(0, 1), (1, 0)])

    columns = 4 * shared + 2 * width
    order, send, low_part = call(
        start_kernel,
        [shape((tokens, tokens), bf16), shape((pairs, lanes, peer, columns), bf16), shape((rank, tokens), f32)],
        (me,),
        (
            tile_slot.reshape(tiles, 1, tokens),
            key_base,
            value_base,
            query_base,
            grad_out,
            hidden_in,
            adapter_down.T,
        ),
        [pl.BlockSpec((1, 1, tokens), lambda i, me: (me[0], 0, 0))] + [None] * 6,
        START_BYTES,
    )
    first = swap(send.reshape(tiles, peer, columns), SEQ)
    low_parts = lax.all_gather(low_part, "tp")
    second_send = call(
        second_kernel,
        shape((pairs, lanes, peer, width + 2 * rank), bf16),
        (),
        (low_parts, hidden_in, order),
    )
    centre = call(
        unpack_kernel,
        shape((2 * tokens, 2 * shared), bf16),
        (),
        (first, second_send),
        [pl.BlockSpec((tiles, peer, 4 * shared), lambda i, *_: (0, 0, 0)), pl.BlockSpec(memory_space=pl.ANY)],
    )
    left, right = shifted(centre, 1), shifted(centre, -1)
    second = swap(second_send.reshape(tiles, peer, width + 2 * rank), SEQ)
    query_tile, grad_tile, hidden_tile, low_tile = call(
        lambda lane, first, second, up, *outs: query_kernel(first, second, up, lane, *outs),
        [shape((tokens, width), bf16)] * 3 + [shape((tokens, 2 * rank), bf16)],
        (lane,),
        (first, second, adapter_up),
    )
    out_tile, low_grad_parts, up_part = call(
        functools.partial(attend_kernel, tiles),
        [shape((tokens, width), bf16), shape((lanes * group, rank, tokens), bf16), shape((rank, width), f32)],
        (lane, window, other_window),
        (left, right, centre, query_tile, grad_tile, low_tile, adapter_up),
    )
    low_grad_parts = swap(low_grad_parts, ("lane", "tp"))
    back_send = call(
        down_kernel,
        shape((tiles, peer, 2 * width), bf16),
        (),
        (low_grad_parts, hidden_tile, out_tile, up_part),
    )
    back = swap(back_send, SEQ)
    totals = swap(call(sum_kernel, shape((tiles, peer, width), bf16), (), (back,)), SEQ)
    attended = call(
        restore_kernel,
        shape((tokens, width), bf16),
        (),
        (order, back.reshape(pairs, lanes, peer, 2 * width)),
    )
    up_total, down_total = call(split_kernel, [shape((rank, width), f32)] * 2, (), (totals,))
    return attended, down_total.T, up_total


def solution(mesh):
    tiles, group = mesh.devices.shape
    lanes = len(HEADS_OF)
    return jax.shard_map(
        local,
        mesh=Mesh(mesh.devices.reshape(tiles // lanes, lanes, group), ("pair", "lane", "tp")),
        in_specs=(
            P(SEQ, "tp"),
            P(SEQ, "tp"),
            P(SEQ, "tp"),
            P(SEQ, "tp"),
            P(SEQ, "tp"),
            P("tp", None),
            P(None, "tp"),
            P(),
            P(SEQ, None),
        ),
        out_specs=(P(SEQ, "tp"), P("tp", None), P(None, "tp")),
        check_vma=False,
    )
```

```python
import functools
import math

import jax
import jax.numpy as jnp
from jax import lax
from jax.experimental import pallas as pl
from jax.experimental.pallas import tpu as pltpu
from jax.sharding import Mesh
from jax.sharding import PartitionSpec as P

HEAD_DIM = 128
REACH = 2
FIRST = ('base', 'grad')
SECOND = ('hidden',)
VMEM_BYTES = 48 * 1024 * 1024
START_BYTES = 60 * 1024 * 1024
SEQ = ("pair", "lane")
HEADS_OF = ((0, 1, 2), (3, 4, 2))
UNITS = ((0, 0), (0, 1), (1, 0), (1, 1), (2, None))
NT = (((1,), (1,)), ((), ()))
NN = (((1,), (0,)), ((), ()))
TN = (((0,), (0,)), ((), ()))


def product(left, right, dims=NN):
    return lax.dot_general(left, right, dims, preferred_element_type=jnp.float32)


def shifted(shard, by):
    devices = lax.axis_size("pair")
    return lax.ppermute(shard, "pair", [(i, (i + by) % devices) for i in range(devices)])


def swap(blocks, axis):
    return lax.all_to_all(blocks, axis, split_axis=0, concat_axis=0, tiled=True)


def call(body, out_shape, prefetch=(), operands=(), in_specs=None, vmem=VMEM_BYTES):
    def whole(shape):
        return pl.BlockSpec(shape, lambda i, *_: (0,) * len(shape))

    specs = in_specs or [None] * len(operands)
    return pl.pallas_call(
        body,
        out_shape=out_shape,
        grid_spec=pltpu.PrefetchScalarGridSpec(
            num_scalar_prefetch=len(prefetch),
            grid=(1,),
            in_specs=[s or whole(o.shape) for s, o in zip(specs, operands)],
            out_specs=jax.tree.map(lambda o: whole(o.shape), out_shape),
        ),
        compiler_params=pltpu.CompilerParams(vmem_limit_bytes=vmem),
    )(*prefetch, *operands)


def head(array, index):
    return array[:, index * HEAD_DIM : (index + 1) * HEAD_DIM]


def place_rows(name, moved, put, start, lanes):
    for lane in range(lanes):
        if name == "hidden":
            put(lane, start, moved[lane])
        else:
            for unit, (j, tile) in enumerate(UNITS):
                put(lane, start + unit * HEAD_DIM, head(moved[lane if tile is None else tile], HEADS_OF[lane][j]))


def start_kernel(tiles, me, slots, window, key, value, hidden, down_t, *refs):
    *others, order, send, part = refs
    tokens = order.shape[0]
    pairs, lanes, peer, _ = send.shape
    width = key.shape[1]
    part[...] = product(down_t[...], hidden[...], NT).astype(part.dtype)
    target = slots[0] // tokens
    rows = lax.broadcasted_iota(jnp.int32, (tokens, tokens), 0)
    cols = lax.broadcasted_iota(jnp.int32, (tokens, tokens), 1)
    spread = jnp.broadcast_to(target, (tokens, tokens))
    target_col = jnp.sum(jnp.where(rows == cols, spread, 0), axis=1, keepdims=True)
    earlier = jnp.logical_and(target_col == spread, rows < cols)
    rank = jnp.sum(jnp.where(earlier, 1, 0), axis=0, keepdims=True)
    half = pairs * peer
    place = lax.rem(target, lanes) * half + lax.div(target, jnp.int32(lanes)) * peer + rank
    one_hot = jnp.where(rows == place, 1.0, 0.0).astype(jnp.bfloat16)
    order[...] = one_hot

    def by_tile(source):
        moved = product(one_hot, source[...]).astype(jnp.bfloat16)
        return [moved[k * half : (k + 1) * half] for k in range(lanes)]

    def put(lane, start, block):
        send[:, lane, :, start : start + block.shape[1]] = block.reshape(pairs, peer, block.shape[1])

    shared = len(HEADS_OF[0]) * HEAD_DIM
    for k, source in enumerate((key, value)):
        moved = by_tile(source)
        for lane in range(lanes):
            for tile in range(lanes):
                for j, h in enumerate(HEADS_OF[lane]):
                    put(lane, (2 * tile + k) * shared + j * HEAD_DIM, head(moved[tile], h))
    start = 2 * lanes * shared
    for name, source in zip(FIRST, others):
        place_rows(name, by_tile(source), put, start, lanes)
        start += width
    away = lax.rem(window[...] - me[0] + tiles, tiles)
    listed = jnp.where(away <= REACH, away + REACH, away - (tiles - REACH))
    missing = 5 * REACH - jnp.sum(listed, axis=1, keepdims=True)
    noted = jnp.broadcast_to(missing.astype(jnp.float32), (half, HEAD_DIM)).astype(jnp.bfloat16)
    for lane in range(lanes):
        put(lane, start, noted)


def add_up(parts):
    total = parts[0].astype(jnp.float32)
    for k in range(1, parts.shape[0]):
        total = total + parts[k].astype(jnp.float32)
    return total.astype(jnp.bfloat16)


def second_kernel(parts, order, *refs):
    *others, send = refs
    pairs, lanes, peer, _ = send.shape
    half = pairs * peer
    one_hot = order[...]

    def by_tile(product_of):
        moved = product_of.astype(jnp.bfloat16)
        return [moved[k * half : (k + 1) * half] for k in range(lanes)]

    def put(lane, start, block):
        send[:, lane, :, start : start + block.shape[1]] = block.reshape(pairs, peer, block.shape[1])

    start = 0
    for name, source in zip(SECOND, others):
        place_rows(name, by_tile(product(one_hot, source[...])), put, start, lanes)
        start += source.shape[1]
    low = jnp.concatenate(by_tile(product(one_hot, add_up(parts), NT)), axis=1)
    for lane in range(lanes):
        put(lane, start, low)


def unpack_kernel(received, after, key_value):
    tokens, width = key_value.shape[0] // 2, key_value.shape[1]
    for tile in range(2):
        key_value[tile * tokens : (tile + 1) * tokens, :] = received[:, :, tile * width : (tile + 1) * width].reshape(
            tokens, width
        )


def own_heads(up, own):
    return [jnp.where(own, head(up, a), head(up, b)) for a, b in zip(*HEADS_OF)]


def attend_kernel(me, left, right, centre, first, second, up, out, low_parts, up_part):
    tokens, width = out.shape
    rank = up.shape[0]
    lane = lax.rem(me[0], 2)
    own = lane == 0
    low_start = second.shape[2] - 2 * rank
    low = second[:, :, low_start : low_start + 2 * rank].reshape(tokens, 2 * rank)
    noted = [first[pl.ds(me[0] - lane + tile, 1), :, first.shape[2] - HEAD_DIM :] for tile in range(2)]
    missing = [jnp.max(note.astype(jnp.float32)).astype(jnp.int32) for note in noted]

    def unit_of(name, at):
        start = first.shape[2] - HEAD_DIM - (len(FIRST) - FIRST.index(name)) * width
        return first[:, :, start + at.start : start + at.stop].reshape(tokens, HEAD_DIM)

    span = [(array, tile) for array in (left, centre, right) for tile in range(2)]

    def block(index, columns):
        array, tile = span[index]
        return array[tile * tokens : (tile + 1) * tokens, columns]

    def chosen(tile, columns):
        if tile is None:
            skip = jnp.where(own, missing[0], missing[1])
            blocks = []
            for k in range(4):
                near = jnp.where(own, block(k, columns), block(k + 1, columns))
                far = jnp.where(own, block(k + 1, columns), block(k + 2, columns))
                blocks.append(jnp.where(skip <= k, far, near))
            return jnp.concatenate(blocks, axis=0)
        return jnp.concatenate(
            [
                jnp.where(missing[tile] <= k, block(tile + k + 1, columns), block(tile + k, columns))
                for k in range(4)
            ],
            axis=0,
        )

    scale = 1.0 / math.sqrt(HEAD_DIM)
    ups = own_heads(up, own)
    low_own = jnp.where(own, low[:, :rank], low[:, rank:])
    low_of = [jnp.zeros((rank, tokens), jnp.float32) for _ in range(2)]
    up_of = [jnp.zeros((rank, HEAD_DIM), jnp.float32) for _ in ups]
    shared = len(ups) * HEAD_DIM
    places = [slice(unit * HEAD_DIM, (unit + 1) * HEAD_DIM) for unit in range(len(UNITS))]
    keys = [chosen(tile, slice(j * HEAD_DIM, (j + 1) * HEAD_DIM)) for j, tile in UNITS]
    values = [chosen(tile, slice(shared + j * HEAD_DIM, shared + (j + 1) * HEAD_DIM)) for j, tile in UNITS]
    lows = [low_own if tile is None else low[:, tile * rank : (tile + 1) * rank] for _, tile in UNITS]
    queries = [
        (unit_of("base", at).astype(jnp.float32) + product(rows, ups[j])).astype(jnp.bfloat16)
        for at, rows, (j, _) in zip(places, lows, UNITS)
    ]
    scores = [product(query, k, NT) * scale for query, k in zip(queries, keys)]
    grad_weights = [product(unit_of("grad", at), v, NT) for at, v in zip(places, values)]
    weights, grad_scores = [], []
    for score, grad_weight in zip(scores, grad_weights):
        exps = jnp.exp(score - jnp.max(score, axis=-1, keepdims=True))
        weight = exps * (1.0 / jnp.sum(exps, axis=-1, keepdims=True))
        row_dot = jnp.sum(weight * grad_weight, axis=-1, keepdims=True)
        grad_scores.append((weight * (grad_weight - row_dot)).astype(jnp.bfloat16))
        weights.append(weight.astype(jnp.bfloat16))
    for at, weight, value in zip(places, weights, values):
        out[:, at] = product(weight, value).astype(jnp.bfloat16)
    grad_queries = [(product(g, k) * scale).astype(jnp.bfloat16) for g, k in zip(grad_scores, keys)]
    for (j, tile), rows, grad_query in zip(UNITS, lows, grad_queries):
        low_grad = product(ups[j], grad_query, NT)
        up_of[j] = up_of[j] + product(rows, grad_query, TN)
        if tile is None:
            low_of = [
                low_of[0] + jnp.where(own, low_grad, 0.0),
                low_of[1] + jnp.where(own, 0.0, low_grad),
            ]
        else:
            low_of[tile] = low_of[tile] + low_grad
    group = low_parts.shape[0] // 2
    for k in range(low_parts.shape[0]):
        low_parts[k] = low_of[k // group].astype(low_parts.dtype)
    for h in range(up_part.shape[1] // HEAD_DIM):
        halves = [up_of[heads.index(h)] if h in heads else jnp.zeros_like(up_of[0]) for heads in HEADS_OF]
        up_part[:, h * HEAD_DIM : (h + 1) * HEAD_DIM] = jnp.where(own, halves[0], halves[1])


def down_kernel(parts, second, out, up_part, send):
    tokens, width = out.shape
    peers, peer, _ = send.shape
    start = SECOND.index("hidden") * width
    down_part = product(add_up(parts), second[:, :, start : start + width].reshape(tokens, width))
    sums = jnp.concatenate([up_part[...], down_part], axis=0).astype(jnp.bfloat16)
    send[:, :, :width] = out[...].reshape(peers, peer, width)
    send[:, :, width:] = sums.reshape(peers, peer, width)


def sum_kernel(received, totals):
    peers, peer, width = totals.shape
    count = peers * peer
    rows = lax.broadcasted_iota(jnp.int32, (count, count), 0)
    cols = lax.broadcasted_iota(jnp.int32, (count, count), 1)
    same = jnp.where(lax.rem(rows, peer) == lax.rem(cols, peer), 1.0, 0.0).astype(jnp.bfloat16)
    total = product(same, received[:, :, width:].reshape(count, width))
    totals[...] = total.astype(totals.dtype).reshape(peers, peer, width)


def restore_kernel(order, received, attended):
    tokens, width = attended.shape
    pairs, lanes, peer, _ = received.shape
    tiles = []
    for tile in range(lanes):
        blocks = []
        for h in range(width // HEAD_DIM):
            for lane, heads in enumerate(HEADS_OF):
                for unit, (j, at) in enumerate(UNITS):
                    if heads[j] == h and (lane if at is None else at) == tile:
                        columns = slice(unit * HEAD_DIM, (unit + 1) * HEAD_DIM)
                        blocks.append(received[:, lane, :, columns].reshape(pairs * peer, HEAD_DIM))
        tiles.append(jnp.concatenate(blocks, axis=1))
    attended[...] = product(order[...], jnp.concatenate(tiles, axis=0), TN).astype(jnp.bfloat16)


def split_kernel(totals, up_total, down_total):
    rank, width = up_total.shape
    rows = totals[...].reshape(2 * rank, width).astype(jnp.float32)
    up_total[...] = rows[:rank]
    down_total[...] = rows[rank:]


def local(
    hidden_in,
    query_base,
    key_base,
    value_base,
    grad_out,
    adapter_down,
    adapter_up,
    tile_slot,
    window_table,
):
    tokens, width = hidden_in.shape
    rank = adapter_up.shape[0]
    tiles = lax.axis_size(SEQ)
    lanes = lax.axis_size("lane")
    pairs = tiles // lanes
    group = lax.axis_size("tp")
    peer = tokens // tiles
    shared = len(HEADS_OF[0]) * HEAD_DIM
    bf16, f32 = jnp.bfloat16, jnp.float32
    shape = jax.ShapeDtypeStruct
    me = lax.axis_index(SEQ).astype(jnp.int32).reshape(1)

    columns = 4 * shared + len(FIRST) * width + HEAD_DIM
    named = {"base": query_base, "grad": grad_out, "hidden": hidden_in}
    order, send, low_part = call(
        functools.partial(start_kernel, tiles),
        [
            shape((tokens, tokens), bf16),
            shape((pairs, lanes, peer, columns), bf16),
            shape((rank, tokens), f32),
        ],
        (me,),
        (
            tile_slot.reshape(tiles, 1, tokens),
            window_table,
            key_base,
            value_base,
            hidden_in,
            adapter_down.T,
            *(named[name] for name in FIRST if name != "hidden"),
        ),
        [pl.BlockSpec((1, 1, tokens), lambda i, me: (me[0], 0, 0))] + [None] * (5 + len(FIRST) - ("hidden" in FIRST)),
        START_BYTES,
    )
    first = swap(send.reshape(tiles, peer, columns), SEQ)
    low_parts = lax.all_gather(low_part, "tp")
    second_width = len(SECOND) * width + 2 * rank
    second_send = call(
        second_kernel,
        shape((pairs, lanes, peer, second_width), bf16),
        (),
        (low_parts, order, *(named[name] for name in SECOND)),
    )
    centre = call(
        unpack_kernel,
        shape((2 * tokens, 2 * shared), bf16),
        (),
        (first, second_send),
        [pl.BlockSpec((tiles, peer, 4 * shared), lambda i, *_: (0, 0, 0)), pl.BlockSpec(memory_space=pl.ANY)],
    )
    left, right = shifted(centre, 1), shifted(centre, -1)
    second = swap(second_send.reshape(tiles, peer, second_width), SEQ)
    out_tile, low_grad_parts, up_part = call(
        attend_kernel,
        [shape((tokens, width), bf16), shape((lanes * group, rank, tokens), bf16), shape((rank, width), f32)],
        (me,),
        (left, right, centre, first, second, adapter_up),
    )
    low_grad_parts = swap(low_grad_parts, ("lane", "tp"))
    back_send = call(
        down_kernel,
        shape((tiles, peer, 2 * width), bf16),
        (),
        (low_grad_parts, second, out_tile, up_part),
    )
    back = swap(back_send, SEQ)
    totals = swap(call(sum_kernel, shape((tiles, peer, width), bf16), (), (back,)), SEQ)
    attended = call(
        restore_kernel,
        shape((tokens, width), bf16),
        (),
        (order, back.reshape(pairs, lanes, peer, 2 * width)),
    )
    up_total, down_total = call(split_kernel, [shape((rank, width), f32)] * 2, (), (totals,))
    return attended, down_total.T, up_total


def solution(mesh):
    tiles, group = mesh.devices.shape
    lanes = len(HEADS_OF)
    return jax.shard_map(
        local,
        mesh=Mesh(mesh.devices.reshape(tiles // lanes, lanes, group), ("pair", "lane", "tp")),
        in_specs=(
            P(SEQ, "tp"),
            P(SEQ, "tp"),
            P(SEQ, "tp"),
            P(SEQ, "tp"),
            P(SEQ, "tp"),
            P("tp", None),
            P(None, "tp"),
            P(),
            P(SEQ, None),
        ),
        out_specs=(P(SEQ, "tp"), P("tp", None), P(None, "tp")),
        check_vma=False,
    )
```

```python
import functools
import math

import jax
import jax.numpy as jnp
from jax import lax
from jax.experimental import pallas as pl
from jax.experimental.pallas import tpu as pltpu
from jax.sharding import Mesh
from jax.sharding import PartitionSpec as P

HEAD_DIM = 128
REACH = 2
FIRST = ('base', 'grad')
SECOND = ('hidden',)
VMEM_BYTES = 48 * 1024 * 1024
START_BYTES = 60 * 1024 * 1024
SEQ = ("pair", "lane")
HEADS_OF = ((0, 1, 2), (3, 4, 2))
UNITS = ((0, 0), (0, 1), (1, 0), (1, 1), (2, None))
NT = (((1,), (1,)), ((), ()))
NN = (((1,), (0,)), ((), ()))
TN = (((0,), (0,)), ((), ()))


def product(left, right, dims=NN):
    return lax.dot_general(left, right, dims, preferred_element_type=jnp.float32)


def shifted(shard, by):
    devices = lax.axis_size("pair")
    return lax.ppermute(shard, "pair", [(i, (i + by) % devices) for i in range(devices)])


def swap(blocks, axis):
    return lax.all_to_all(blocks, axis, split_axis=0, concat_axis=0, tiled=True)


def call(body, out_shape, prefetch=(), operands=(), in_specs=None, vmem=VMEM_BYTES):
    def whole(shape):
        return pl.BlockSpec(shape, lambda i, *_: (0,) * len(shape))

    specs = in_specs or [None] * len(operands)
    return pl.pallas_call(
        body,
        out_shape=out_shape,
        grid_spec=pltpu.PrefetchScalarGridSpec(
            num_scalar_prefetch=len(prefetch),
            grid=(1,),
            in_specs=[s or whole(o.shape) for s, o in zip(specs, operands)],
            out_specs=jax.tree.map(lambda o: whole(o.shape), out_shape),
        ),
        compiler_params=pltpu.CompilerParams(vmem_limit_bytes=vmem),
    )(*prefetch, *operands)


def head(array, index):
    return array[:, index * HEAD_DIM : (index + 1) * HEAD_DIM]


def place_rows(name, moved, put, start, lanes):
    for lane in range(lanes):
        if name == "hidden":
            put(lane, start, moved[lane])
        else:
            for unit, (j, tile) in enumerate(UNITS):
                put(lane, start + unit * HEAD_DIM, head(moved[lane if tile is None else tile], HEADS_OF[lane][j]))


def start_kernel(tiles, me, slots, window, key, value, hidden, down_t, *refs):
    *others, order, send, part = refs
    tokens = order.shape[0]
    pairs, lanes, peer, _ = send.shape
    width = key.shape[1]
    part[...] = product(down_t[...], hidden[...], NT).astype(part.dtype)
    target = slots[0] // tokens
    rows = lax.broadcasted_iota(jnp.int32, (tokens, tokens), 0)
    cols = lax.broadcasted_iota(jnp.int32, (tokens, tokens), 1)
    spread = jnp.broadcast_to(target, (tokens, tokens))
    target_col = jnp.sum(jnp.where(rows == cols, spread, 0), axis=1, keepdims=True)
    earlier = jnp.logical_and(target_col == spread, rows < cols)
    rank = jnp.sum(jnp.where(earlier, 1, 0), axis=0, keepdims=True)
    half = pairs * peer
    place = lax.rem(target, lanes) * half + lax.div(target, jnp.int32(lanes)) * peer + rank
    one_hot = jnp.where(rows == place, 1.0, 0.0).astype(jnp.bfloat16)
    order[...] = one_hot

    def by_tile(source):
        moved = product(one_hot, source[...]).astype(jnp.bfloat16)
        return [moved[k * half : (k + 1) * half] for k in range(lanes)]

    def put(lane, start, block):
        send[:, lane, :, start : start + block.shape[1]] = block.reshape(pairs, peer, block.shape[1])

    shared = len(HEADS_OF[0]) * HEAD_DIM
    for k, source in enumerate((key, value)):
        moved = by_tile(source)
        for lane in range(lanes):
            for tile in range(lanes):
                for j, h in enumerate(HEADS_OF[lane]):
                    put(lane, (2 * tile + k) * shared + j * HEAD_DIM, head(moved[tile], h))
    start = 2 * lanes * shared
    for name, source in zip(FIRST, others):
        place_rows(name, by_tile(source), put, start, lanes)
        start += width
    away = lax.rem(window[...] - me[0] + tiles, tiles)
    listed = jnp.where(away <= REACH, away + REACH, away - (tiles - REACH))
    missing = 5 * REACH - jnp.sum(listed, axis=1, keepdims=True)
    noted = jnp.broadcast_to(missing.astype(jnp.float32), (half, HEAD_DIM)).astype(jnp.bfloat16)
    for lane in range(lanes):
        put(lane, start, noted)


def add_up(parts):
    total = parts[0].astype(jnp.float32)
    for k in range(1, parts.shape[0]):
        total = total + parts[k].astype(jnp.float32)
    return total.astype(jnp.bfloat16)


def second_kernel(parts, order, *refs):
    *others, send = refs
    pairs, lanes, peer, _ = send.shape
    half = pairs * peer
    one_hot = order[...]

    def by_tile(product_of):
        moved = product_of.astype(jnp.bfloat16)
        return [moved[k * half : (k + 1) * half] for k in range(lanes)]

    def put(lane, start, block):
        send[:, lane, :, start : start + block.shape[1]] = block.reshape(pairs, peer, block.shape[1])

    start = 0
    for name, source in zip(SECOND, others):
        place_rows(name, by_tile(product(one_hot, source[...])), put, start, lanes)
        start += source.shape[1]
    low = jnp.concatenate(by_tile(product(one_hot, add_up(parts), NT)), axis=1)
    for lane in range(lanes):
        put(lane, start, low)


def unpack_kernel(received, after, key_value):
    tokens, width = key_value.shape[0] // 2, key_value.shape[1]
    for tile in range(2):
        key_value[tile * tokens : (tile + 1) * tokens, :] = received[:, :, tile * width : (tile + 1) * width].reshape(
            tokens, width
        )


def own_heads(up, own):
    return [jnp.where(own, head(up, a), head(up, b)) for a, b in zip(*HEADS_OF)]


def attend_kernel(me, left, right, centre, first, second, up, out, low_parts, up_part):
    tokens, width = out.shape
    rank = up.shape[0]
    lane = lax.rem(me[0], 2)
    own = lane == 0
    low_start = second.shape[2] - 2 * rank
    low = second[:, :, low_start : low_start + 2 * rank].reshape(tokens, 2 * rank)
    noted = [first[pl.ds(me[0] - lane + tile, 1), :, first.shape[2] - HEAD_DIM :] for tile in range(2)]
    missing = [jnp.max(note.astype(jnp.float32)).astype(jnp.int32) for note in noted]

    def unit_of(name, at):
        start = first.shape[2] - HEAD_DIM - (len(FIRST) - FIRST.index(name)) * width
        return first[:, :, start + at.start : start + at.stop].reshape(tokens, HEAD_DIM)

    span = [(array, tile) for array in (left, centre, right) for tile in range(2)]

    def block(index, columns):
        array, tile = span[index]
        return array[tile * tokens : (tile + 1) * tokens, columns]

    def chosen(tile, columns):
        if tile is None:
            skip = jnp.where(own, missing[0], missing[1])
            blocks = []
            for k in range(4):
                near = jnp.where(own, block(k, columns), block(k + 1, columns))
                far = jnp.where(own, block(k + 1, columns), block(k + 2, columns))
                blocks.append(jnp.where(skip <= k, far, near))
            return jnp.concatenate(blocks, axis=0)
        return jnp.concatenate(
            [
                jnp.where(missing[tile] <= k, block(tile + k + 1, columns), block(tile + k, columns))
                for k in range(4)
            ],
            axis=0,
        )

    scale = 1.0 / math.sqrt(HEAD_DIM)
    ups = own_heads(up, own)
    low_own = jnp.where(own, low[:, :rank], low[:, rank:])
    low_of = [jnp.zeros((rank, tokens), jnp.float32) for _ in range(2)]
    up_of = [jnp.zeros((rank, HEAD_DIM), jnp.float32) for _ in ups]
    shared = len(ups) * HEAD_DIM
    places = [slice(unit * HEAD_DIM, (unit + 1) * HEAD_DIM) for unit in range(len(UNITS))]
    keys = [chosen(tile, slice(j * HEAD_DIM, (j + 1) * HEAD_DIM)) for j, tile in UNITS]
    values = [chosen(tile, slice(shared + j * HEAD_DIM, shared + (j + 1) * HEAD_DIM)) for j, tile in UNITS]
    lows = [low_own if tile is None else low[:, tile * rank : (tile + 1) * rank] for _, tile in UNITS]
    queries = [
        (unit_of("base", at).astype(jnp.float32) + product(rows, ups[j])).astype(jnp.bfloat16)
        for at, rows, (j, _) in zip(places, lows, UNITS)
    ]
    scores = [product(query, k, NT) * scale for query, k in zip(queries, keys)]
    grad_weights = [product(unit_of("grad", at), v, NT) for at, v in zip(places, values)]
    weights, grad_scores = [], []
    for score, grad_weight in zip(scores, grad_weights):
        exps = jnp.exp(score - jnp.max(score, axis=-1, keepdims=True))
        weight = exps * (1.0 / jnp.sum(exps, axis=-1, keepdims=True))
        row_dot = jnp.sum(weight * grad_weight, axis=-1, keepdims=True)
        grad_scores.append((weight * (grad_weight - row_dot)).astype(jnp.bfloat16))
        weights.append(weight.astype(jnp.bfloat16))
    for at, weight, value in zip(places, weights, values):
        out[:, at] = product(weight, value).astype(jnp.bfloat16)
    grad_queries = [(product(g, k) * scale).astype(jnp.bfloat16) for g, k in zip(grad_scores, keys)]
    for (j, tile), rows, grad_query in zip(UNITS, lows, grad_queries):
        low_grad = product(ups[j], grad_query, NT)
        up_of[j] = up_of[j] + product(rows, grad_query, TN)
        if tile is None:
            low_of = [
                low_of[0] + jnp.where(own, low_grad, 0.0),
                low_of[1] + jnp.where(own, 0.0, low_grad),
            ]
        else:
            low_of[tile] = low_of[tile] + low_grad
    group = low_parts.shape[0] // 2
    for k in range(low_parts.shape[0]):
        low_parts[k] = low_of[k // group].astype(low_parts.dtype)
    for h in range(up_part.shape[1] // HEAD_DIM):
        halves = [up_of[heads.index(h)] if h in heads else jnp.zeros_like(up_of[0]) for heads in HEADS_OF]
        up_part[:, h * HEAD_DIM : (h + 1) * HEAD_DIM] = jnp.where(own, halves[0], halves[1])


def down_kernel(parts, second, out, up_part, send):
    tokens, width = out.shape
    peers, peer, _ = send.shape
    start = SECOND.index("hidden") * width
    down_part = product(add_up(parts), second[:, :, start : start + width].reshape(tokens, width))
    sums = jnp.concatenate([up_part[...], down_part], axis=0).astype(jnp.bfloat16)
    send[:, :, :width] = out[...].reshape(peers, peer, width)
    send[:, :, width:] = sums.reshape(peers, peer, width)


def sum_kernel(received, totals):
    peers, peer, width = totals.shape
    count = peers * peer
    rows = lax.broadcasted_iota(jnp.int32, (count, count), 0)
    cols = lax.broadcasted_iota(jnp.int32, (count, count), 1)
    same = jnp.where(lax.rem(rows, peer) == lax.rem(cols, peer), 1.0, 0.0).astype(jnp.bfloat16)
    total = product(same, received[:, :, width:].reshape(count, width))
    totals[...] = total.astype(totals.dtype).reshape(peers, peer, width)


def finish_kernel(order, received, totals, attended, up_total, down_total):
    rank = up_total.shape[0]
    tokens, width = attended.shape
    pairs, lanes, peer, _ = received.shape
    tiles = []
    for tile in range(lanes):
        blocks = []
        for h in range(width // HEAD_DIM):
            for lane, heads in enumerate(HEADS_OF):
                for unit, (j, at) in enumerate(UNITS):
                    if heads[j] == h and (lane if at is None else at) == tile:
                        columns = slice(unit * HEAD_DIM, (unit + 1) * HEAD_DIM)
                        blocks.append(received[:, lane, :, columns].reshape(pairs * peer, HEAD_DIM))
        tiles.append(jnp.concatenate(blocks, axis=1))
    attended[...] = product(order[...], jnp.concatenate(tiles, axis=0), TN).astype(jnp.bfloat16)
    sums = totals[...].reshape(2 * rank, width).astype(jnp.float32)
    up_total[...] = sums[:rank]
    down_total[...] = sums[rank:]


def local(
    hidden_in,
    query_base,
    key_base,
    value_base,
    grad_out,
    adapter_down,
    adapter_up,
    tile_slot,
    window_table,
):
    tokens, width = hidden_in.shape
    rank = adapter_up.shape[0]
    tiles = lax.axis_size(SEQ)
    lanes = lax.axis_size("lane")
    pairs = tiles // lanes
    group = lax.axis_size("tp")
    peer = tokens // tiles
    shared = len(HEADS_OF[0]) * HEAD_DIM
    bf16, f32 = jnp.bfloat16, jnp.float32
    shape = jax.ShapeDtypeStruct
    me = lax.axis_index(SEQ).astype(jnp.int32).reshape(1)

    columns = 4 * shared + len(FIRST) * width + HEAD_DIM
    named = {"base": query_base, "grad": grad_out, "hidden": hidden_in}
    order, send, low_part = call(
        functools.partial(start_kernel, tiles),
        [
            shape((tokens, tokens), bf16),
            shape((pairs, lanes, peer, columns), bf16),
            shape((rank, tokens), f32),
        ],
        (me,),
        (
            tile_slot.reshape(tiles, 1, tokens),
            window_table,
            key_base,
            value_base,
            hidden_in,
            adapter_down.T,
            *(named[name] for name in FIRST if name != "hidden"),
        ),
        [pl.BlockSpec((1, 1, tokens), lambda i, me: (me[0], 0, 0))] + [None] * (5 + len(FIRST) - ("hidden" in FIRST)),
        START_BYTES,
    )
    first = swap(send.reshape(tiles, peer, columns), SEQ)
    low_parts = lax.all_gather(low_part, "tp")
    second_width = len(SECOND) * width + 2 * rank
    second_send = call(
        second_kernel,
        shape((pairs, lanes, peer, second_width), bf16),
        (),
        (low_parts, order, *(named[name] for name in SECOND)),
    )
    centre = call(
        unpack_kernel,
        shape((2 * tokens, 2 * shared), bf16),
        (),
        (first, second_send),
        [pl.BlockSpec((tiles, peer, 4 * shared), lambda i, *_: (0, 0, 0)), pl.BlockSpec(memory_space=pl.ANY)],
    )
    left, right = shifted(centre, 1), shifted(centre, -1)
    second = swap(second_send.reshape(tiles, peer, second_width), SEQ)
    out_tile, low_grad_parts, up_part = call(
        attend_kernel,
        [shape((tokens, width), bf16), shape((lanes * group, rank, tokens), bf16), shape((rank, width), f32)],
        (me,),
        (left, right, centre, first, second, adapter_up),
    )
    low_grad_parts = swap(low_grad_parts, ("lane", "tp"))
    back_send = call(
        down_kernel,
        shape((tiles, peer, 2 * width), bf16),
        (),
        (low_grad_parts, second, out_tile, up_part),
    )
    back = swap(back_send, SEQ)
    totals = swap(call(sum_kernel, shape((tiles, peer, width), bf16), (), (back,)), SEQ)
    attended, up_total, down_total = call(
        finish_kernel,
        [shape((tokens, width), bf16)] + [shape((rank, width), f32)] * 2,
        (),
        (order, back.reshape(pairs, lanes, peer, 2 * width), totals),
    )
    return attended, down_total.T, up_total


def solution(mesh):
    tiles, group = mesh.devices.shape
    lanes = len(HEADS_OF)
    return jax.shard_map(
        local,
        mesh=Mesh(mesh.devices.reshape(tiles // lanes, lanes, group), ("pair", "lane", "tp")),
        in_specs=(
            P(SEQ, "tp"),
            P(SEQ, "tp"),
            P(SEQ, "tp"),
            P(SEQ, "tp"),
            P(SEQ, "tp"),
            P("tp", None),
            P(None, "tp"),
            P(),
            P(SEQ, None),
        ),
        out_specs=(P(SEQ, "tp"), P("tp", None), P(None, "tp")),
        check_vma=False,
    )
```

```python
import functools
import math

import jax
import jax.numpy as jnp
from jax import lax
from jax.experimental import pallas as pl
from jax.experimental.pallas import tpu as pltpu
from jax.sharding import Mesh
from jax.sharding import PartitionSpec as P

HEAD_DIM = 128
REACH = 2
FIRST = ('base', 'grad')
SECOND = ('hidden',)
VMEM_BYTES = 48 * 1024 * 1024
START_BYTES = 60 * 1024 * 1024
SEQ = ("pair", "lane")
TP = ("chip", "core")
CORES = 2
HEADS_OF = ((0, 1, 2), (3, 4, 2))
UNITS = ((0, 0), (0, 1), (1, 0), (1, 1), (2, None))
NT = (((1,), (1,)), ((), ()))
NN = (((1,), (0,)), ((), ()))
TN = (((0,), (0,)), ((), ()))


def product(left, right, dims=NN):
    return lax.dot_general(left, right, dims, preferred_element_type=jnp.float32)


def shifted(shard, by):
    devices = lax.axis_size("pair")
    return lax.ppermute(shard, "pair", [(i, (i + by) % devices) for i in range(devices)])


def swap(blocks, axis):
    return lax.all_to_all(blocks, axis, split_axis=0, concat_axis=0, tiled=True)


def call(body, out_shape, prefetch=(), operands=(), in_specs=None, vmem=VMEM_BYTES):
    def whole(shape):
        return pl.BlockSpec(shape, lambda i, *_: (0,) * len(shape))

    specs = in_specs or [None] * len(operands)
    return pl.pallas_call(
        body,
        out_shape=out_shape,
        grid_spec=pltpu.PrefetchScalarGridSpec(
            num_scalar_prefetch=len(prefetch),
            grid=(1,),
            in_specs=[s or whole(o.shape) for s, o in zip(specs, operands)],
            out_specs=jax.tree.map(lambda o: whole(o.shape), out_shape),
        ),
        compiler_params=pltpu.CompilerParams(vmem_limit_bytes=vmem),
    )(*prefetch, *operands)


def head(array, index):
    return array[:, index * HEAD_DIM : (index + 1) * HEAD_DIM]


def place_rows(name, moved, put, start, lanes):
    for lane in range(lanes):
        if name == "hidden":
            put(lane, start, moved[lane])
        else:
            for unit, (j, tile) in enumerate(UNITS):
                put(lane, start + unit * HEAD_DIM, head(moved[lane if tile is None else tile], HEADS_OF[lane][j]))


def start_kernel(tiles, me, slots, window, key, value, hidden, down_t, *refs):
    *others, order, send, part = refs
    tokens = order.shape[0]
    pairs, lanes, peer, _ = send.shape
    width = key.shape[1]
    part[...] = product(down_t[...], hidden[...], NT).astype(part.dtype)
    target = slots[0] // tokens
    rows = lax.broadcasted_iota(jnp.int32, (tokens, tokens), 0)
    cols = lax.broadcasted_iota(jnp.int32, (tokens, tokens), 1)
    spread = jnp.broadcast_to(target, (tokens, tokens))
    target_col = jnp.sum(jnp.where(rows == cols, spread, 0), axis=1, keepdims=True)
    earlier = jnp.logical_and(target_col == spread, rows < cols)
    rank = jnp.sum(jnp.where(earlier, 1, 0), axis=0, keepdims=True)
    half = pairs * peer
    place = lax.rem(target, lanes) * half + lax.div(target, jnp.int32(lanes)) * peer + rank
    one_hot = jnp.where(rows == place, 1.0, 0.0).astype(jnp.bfloat16)
    order[...] = one_hot

    def by_tile(source):
        moved = product(one_hot, source[...]).astype(jnp.bfloat16)
        return [moved[k * half : (k + 1) * half] for k in range(lanes)]

    def put(lane, start, block):
        send[:, lane, :, start : start + block.shape[1]] = block.reshape(pairs, peer, block.shape[1])

    shared = len(HEADS_OF[0]) * HEAD_DIM
    for k, source in enumerate((key, value)):
        moved = by_tile(source)
        for lane in range(lanes):
            for tile in range(lanes):
                for j, h in enumerate(HEADS_OF[lane]):
                    put(lane, (2 * tile + k) * shared + j * HEAD_DIM, head(moved[tile], h))
    start = 2 * lanes * shared
    for name, source in zip(FIRST, others):
        place_rows(name, by_tile(source), put, start, lanes)
        start += width
    away = lax.rem(window[...] - me[0] + tiles, tiles)
    listed = jnp.where(away <= REACH, away + REACH, away - (tiles - REACH))
    missing = 5 * REACH - jnp.sum(listed, axis=1, keepdims=True)
    noted = jnp.broadcast_to(missing.astype(jnp.float32), (half, HEAD_DIM)).astype(jnp.bfloat16)
    for lane in range(lanes):
        put(lane, start, noted)


def add_up(parts):
    total = parts[0].astype(jnp.float32)
    for k in range(1, parts.shape[0]):
        total = total + parts[k].astype(jnp.float32)
    return total.astype(jnp.bfloat16)


def second_kernel(parts, order, *refs):
    *others, send = refs
    pairs, lanes, peer, _ = send.shape
    half = pairs * peer
    one_hot = order[...]

    def by_tile(product_of):
        moved = product_of.astype(jnp.bfloat16)
        return [moved[k * half : (k + 1) * half] for k in range(lanes)]

    def put(lane, start, block):
        send[:, lane, :, start : start + block.shape[1]] = block.reshape(pairs, peer, block.shape[1])

    start = 0
    for name, source in zip(SECOND, others):
        place_rows(name, by_tile(product(one_hot, source[...])), put, start, lanes)
        start += source.shape[1]
    low = jnp.concatenate(by_tile(product(one_hot, add_up(parts), NT)), axis=1)
    for lane in range(lanes):
        put(lane, start, low)


def unpack_kernel(received, after, key_value):
    tokens, width = key_value.shape[0] // 2, key_value.shape[1]
    for tile in range(2):
        key_value[tile * tokens : (tile + 1) * tokens, :] = received[:, :, tile * width : (tile + 1) * width].reshape(
            tokens, width
        )


def own_heads(up, own):
    return [jnp.where(own, head(up, a), head(up, b)) for a, b in zip(*HEADS_OF)]


def attend_kernel(me, left, right, centre, first, second, up, out, low_parts, up_part):
    tokens, width = out.shape
    rank = up.shape[0]
    lane = lax.rem(me[0], 2)
    own = lane == 0
    low_start = second.shape[2] - 2 * rank
    low = second[:, :, low_start : low_start + 2 * rank].reshape(tokens, 2 * rank)
    noted = [first[pl.ds(me[0] - lane + tile, 1), :, first.shape[2] - HEAD_DIM :] for tile in range(2)]
    missing = [jnp.max(note.astype(jnp.float32)).astype(jnp.int32) for note in noted]

    def unit_of(name, at):
        start = first.shape[2] - HEAD_DIM - (len(FIRST) - FIRST.index(name)) * width
        return first[:, :, start + at.start : start + at.stop].reshape(tokens, HEAD_DIM)

    span = [(array, tile) for array in (left, centre, right) for tile in range(2)]

    def block(index, columns):
        array, tile = span[index]
        return array[tile * tokens : (tile + 1) * tokens, columns]

    def chosen(tile, columns):
        if tile is None:
            skip = jnp.where(own, missing[0], missing[1])
            blocks = []
            for k in range(4):
                near = jnp.where(own, block(k, columns), block(k + 1, columns))
                far = jnp.where(own, block(k + 1, columns), block(k + 2, columns))
                blocks.append(jnp.where(skip <= k, far, near))
            return jnp.concatenate(blocks, axis=0)
        return jnp.concatenate(
            [
                jnp.where(missing[tile] <= k, block(tile + k + 1, columns), block(tile + k, columns))
                for k in range(4)
            ],
            axis=0,
        )

    scale = 1.0 / math.sqrt(HEAD_DIM)
    ups = own_heads(up, own)
    low_own = jnp.where(own, low[:, :rank], low[:, rank:])
    low_of = [jnp.zeros((rank, tokens), jnp.float32) for _ in range(2)]
    up_of = [jnp.zeros((rank, HEAD_DIM), jnp.float32) for _ in ups]
    shared = len(ups) * HEAD_DIM
    places = [slice(unit * HEAD_DIM, (unit + 1) * HEAD_DIM) for unit in range(len(UNITS))]
    keys = [chosen(tile, slice(j * HEAD_DIM, (j + 1) * HEAD_DIM)) for j, tile in UNITS]
    values = [chosen(tile, slice(shared + j * HEAD_DIM, shared + (j + 1) * HEAD_DIM)) for j, tile in UNITS]
    lows = [low_own if tile is None else low[:, tile * rank : (tile + 1) * rank] for _, tile in UNITS]
    queries = [
        (unit_of("base", at).astype(jnp.float32) + product(rows, ups[j])).astype(jnp.bfloat16)
        for at, rows, (j, _) in zip(places, lows, UNITS)
    ]
    scores = [product(query, k, NT) * scale for query, k in zip(queries, keys)]
    grad_weights = [product(unit_of("grad", at), v, NT) for at, v in zip(places, values)]
    weights, grad_scores = [], []
    for score, grad_weight in zip(scores, grad_weights):
        exps = jnp.exp(score - jnp.max(score, axis=-1, keepdims=True))
        weight = exps * (1.0 / jnp.sum(exps, axis=-1, keepdims=True))
        row_dot = jnp.sum(weight * grad_weight, axis=-1, keepdims=True)
        grad_scores.append((weight * (grad_weight - row_dot)).astype(jnp.bfloat16))
        weights.append(weight.astype(jnp.bfloat16))
    for at, weight, value in zip(places, weights, values):
        out[:, at] = product(weight, value).astype(jnp.bfloat16)
    grad_queries = [(product(g, k) * scale).astype(jnp.bfloat16) for g, k in zip(grad_scores, keys)]
    for (j, tile), rows, grad_query in zip(UNITS, lows, grad_queries):
        low_grad = product(ups[j], grad_query, NT)
        up_of[j] = up_of[j] + product(rows, grad_query, TN)
        if tile is None:
            low_of = [
                low_of[0] + jnp.where(own, low_grad, 0.0),
                low_of[1] + jnp.where(own, 0.0, low_grad),
            ]
        else:
            low_of[tile] = low_of[tile] + low_grad
    for tile in range(2):
        low_parts[tile] = low_of[tile]
    for h in range(up_part.shape[1] // HEAD_DIM):
        halves = [up_of[heads.index(h)] if h in heads else jnp.zeros_like(up_of[0]) for heads in HEADS_OF]
        up_part[:, h * HEAD_DIM : (h + 1) * HEAD_DIM] = jnp.where(own, halves[0], halves[1])


def chip_kernel(parts, send):
    lanes = parts.shape[1]
    chips = send.shape[0] // lanes
    for tile in range(lanes):
        total = (parts[0, tile] + parts[1, tile]).astype(send.dtype)
        for k in range(chips):
            send[tile * chips + k] = total


def down_kernel(parts, second, out, up_part, send):
    tokens, width = out.shape
    peers, peer, _ = send.shape
    start = SECOND.index("hidden") * width
    down_part = product(add_up(parts), second[:, :, start : start + width].reshape(tokens, width))
    sums = jnp.concatenate([up_part[...], down_part], axis=0).astype(jnp.bfloat16)
    send[:, :, :width] = out[...].reshape(peers, peer, width)
    send[:, :, width:] = sums.reshape(peers, peer, width)


def sum_kernel(received, totals):
    peers, peer, width = totals.shape
    count = peers * peer
    rows = lax.broadcasted_iota(jnp.int32, (count, count), 0)
    cols = lax.broadcasted_iota(jnp.int32, (count, count), 1)
    same = jnp.where(lax.rem(rows, peer) == lax.rem(cols, peer), 1.0, 0.0).astype(jnp.bfloat16)
    total = product(same, received[:, :, width:].reshape(count, width))
    totals[...] = total.astype(totals.dtype).reshape(peers, peer, width)


def finish_kernel(order, received, totals, attended, up_total, down_total):
    rank = up_total.shape[0]
    tokens, width = attended.shape
    pairs, lanes, peer, _ = received.shape
    tiles = []
    for tile in range(lanes):
        blocks = []
        for h in range(width // HEAD_DIM):
            for lane, heads in enumerate(HEADS_OF):
                for unit, (j, at) in enumerate(UNITS):
                    if heads[j] == h and (lane if at is None else at) == tile:
                        columns = slice(unit * HEAD_DIM, (unit + 1) * HEAD_DIM)
                        blocks.append(received[:, lane, :, columns].reshape(pairs * peer, HEAD_DIM))
        tiles.append(jnp.concatenate(blocks, axis=1))
    attended[...] = product(order[...], jnp.concatenate(tiles, axis=0), TN).astype(jnp.bfloat16)
    sums = totals[...].reshape(2 * rank, width).astype(jnp.float32)
    up_total[...] = sums[:rank]
    down_total[...] = sums[rank:]


def local(
    hidden_in,
    query_base,
    key_base,
    value_base,
    grad_out,
    adapter_down,
    adapter_up,
    tile_slot,
    window_table,
):
    tokens, width = hidden_in.shape
    rank = adapter_up.shape[0]
    tiles = lax.axis_size(SEQ)
    lanes = lax.axis_size("lane")
    pairs = tiles // lanes
    group = lax.axis_size(TP)
    peer = tokens // tiles
    shared = len(HEADS_OF[0]) * HEAD_DIM
    bf16, f32 = jnp.bfloat16, jnp.float32
    shape = jax.ShapeDtypeStruct
    me = lax.axis_index(SEQ).astype(jnp.int32).reshape(1)

    columns = 4 * shared + len(FIRST) * width + HEAD_DIM
    named = {"base": query_base, "grad": grad_out, "hidden": hidden_in}
    order, send, low_part = call(
        functools.partial(start_kernel, tiles),
        [
            shape((tokens, tokens), bf16),
            shape((pairs, lanes, peer, columns), bf16),
            shape((rank, tokens), f32),
        ],
        (me,),
        (
            tile_slot.reshape(tiles, 1, tokens),
            window_table,
            key_base,
            value_base,
            hidden_in,
            adapter_down.T,
            *(named[name] for name in FIRST if name != "hidden"),
        ),
        [pl.BlockSpec((1, 1, tokens), lambda i, me: (me[0], 0, 0))] + [None] * (5 + len(FIRST) - ("hidden" in FIRST)),
        START_BYTES,
    )
    first = swap(send.reshape(tiles, peer, columns), SEQ)
    low_parts = lax.all_gather(jnp.sum(lax.all_gather(low_part, "core"), axis=0), "chip")
    second_width = len(SECOND) * width + 2 * rank
    second_send = call(
        second_kernel,
        shape((pairs, lanes, peer, second_width), bf16),
        (),
        (low_parts, order, *(named[name] for name in SECOND)),
    )
    centre = call(
        unpack_kernel,
        shape((2 * tokens, 2 * shared), bf16),
        (),
        (first, second_send),
        [pl.BlockSpec((tiles, peer, 4 * shared), lambda i, *_: (0, 0, 0)), pl.BlockSpec(memory_space=pl.ANY)],
    )
    left, right = shifted(centre, 1), shifted(centre, -1)
    second = swap(second_send.reshape(tiles, peer, second_width), SEQ)
    out_tile, low_grad_parts, up_part = call(
        attend_kernel,
        [shape((tokens, width), bf16), shape((lanes, rank, tokens), f32), shape((rank, width), f32)],
        (me,),
        (left, right, centre, first, second, adapter_up),
    )
    low_grad_parts = call(
        chip_kernel,
        shape((lanes * group // CORES, rank, tokens), bf16),
        (),
        (lax.all_gather(low_grad_parts, "core"),),
    )
    low_grad_parts = swap(low_grad_parts, ("lane", "chip"))
    back_send = call(
        down_kernel,
        shape((tiles, peer, 2 * width), bf16),
        (),
        (low_grad_parts, second, out_tile, up_part),
    )
    back = swap(back_send, SEQ)
    totals = swap(call(sum_kernel, shape((tiles, peer, width), bf16), (), (back,)), SEQ)
    attended, up_total, down_total = call(
        finish_kernel,
        [shape((tokens, width), bf16)] + [shape((rank, width), f32)] * 2,
        (),
        (order, back.reshape(pairs, lanes, peer, 2 * width), totals),
    )
    return attended, down_total.T, up_total


def solution(mesh):
    tiles, group = mesh.devices.shape
    lanes = len(HEADS_OF)
    return jax.shard_map(
        local,
        mesh=Mesh(
            mesh.devices.reshape(tiles // lanes, lanes, group // CORES, CORES), ("pair", "lane", "chip", "core")
        ),
        in_specs=(
            P(SEQ, TP),
            P(SEQ, TP),
            P(SEQ, TP),
            P(SEQ, TP),
            P(SEQ, TP),
            P(TP, None),
            P(None, TP),
            P(),
            P(SEQ, None),
        ),
        out_specs=(P(SEQ, TP), P(TP, None), P(None, TP)),
        check_vma=False,
    )
```

```python
import functools
import math

import jax
import jax.numpy as jnp
from jax import lax
from jax.experimental import pallas as pl
from jax.experimental.pallas import tpu as pltpu
from jax.sharding import Mesh
from jax.sharding import PartitionSpec as P

HEAD_DIM = 128
REACH = 2
FIRST = ('base', 'grad')
SECOND = ('hidden',)
VMEM_BYTES = 48 * 1024 * 1024
START_BYTES = 60 * 1024 * 1024
SEQ = ("pair", "lane")
TP = ("chip", "core")
CORES = 2
HEADS_OF = ((0, 1, 2), (3, 4, 2))
UNITS = ((0, 0), (0, 1), (1, 0), (1, 1), (2, None))
NT = (((1,), (1,)), ((), ()))
NN = (((1,), (0,)), ((), ()))
TN = (((0,), (0,)), ((), ()))


def product(left, right, dims=NN):
    return lax.dot_general(left, right, dims, preferred_element_type=jnp.float32)


def shifted(shard, by):
    devices = lax.axis_size("pair")
    return lax.ppermute(shard, "pair", [(i, (i + by) % devices) for i in range(devices)])


def swap(blocks, axis):
    return lax.all_to_all(blocks, axis, split_axis=0, concat_axis=0, tiled=True)


def call(body, out_shape, prefetch=(), operands=(), in_specs=None, vmem=VMEM_BYTES):
    def whole(shape):
        return pl.BlockSpec(shape, lambda i, *_: (0,) * len(shape))

    specs = in_specs or [None] * len(operands)
    return pl.pallas_call(
        body,
        out_shape=out_shape,
        grid_spec=pltpu.PrefetchScalarGridSpec(
            num_scalar_prefetch=len(prefetch),
            grid=(1,),
            in_specs=[s or whole(o.shape) for s, o in zip(specs, operands)],
            out_specs=jax.tree.map(lambda o: whole(o.shape), out_shape),
        ),
        compiler_params=pltpu.CompilerParams(vmem_limit_bytes=vmem),
    )(*prefetch, *operands)


def head(array, index):
    return array[:, index * HEAD_DIM : (index + 1) * HEAD_DIM]


def place_rows(name, moved, put, start, lanes):
    for lane in range(lanes):
        if name == "hidden":
            put(lane, start, moved[lane])
        else:
            for unit, (j, tile) in enumerate(UNITS):
                put(lane, start + unit * HEAD_DIM, head(moved[lane if tile is None else tile], HEADS_OF[lane][j]))


def start_kernel(tiles, me, slots, window, key, value, hidden, down_t, *refs):
    *others, order, send, part = refs
    tokens = order.shape[0]
    pairs, lanes, peer, _ = send.shape
    width = key.shape[1]
    part[...] = product(down_t[...], hidden[...], NT).astype(part.dtype)
    target = slots[0] // tokens
    rows = lax.broadcasted_iota(jnp.int32, (tokens, tokens), 0)
    cols = lax.broadcasted_iota(jnp.int32, (tokens, tokens), 1)
    spread = jnp.broadcast_to(target, (tokens, tokens))
    target_col = jnp.sum(jnp.where(rows == cols, spread, 0), axis=1, keepdims=True)
    earlier = jnp.logical_and(target_col == spread, rows < cols)
    rank = jnp.sum(jnp.where(earlier, 1, 0), axis=0, keepdims=True)
    half = pairs * peer
    place = lax.rem(target, lanes) * half + lax.div(target, jnp.int32(lanes)) * peer + rank
    one_hot = jnp.where(rows == place, 1.0, 0.0).astype(jnp.bfloat16)
    order[...] = one_hot

    def by_tile(source):
        moved = product(one_hot, source[...]).astype(jnp.bfloat16)
        return [moved[k * half : (k + 1) * half] for k in range(lanes)]

    def put(lane, start, block):
        send[:, lane, :, start : start + block.shape[1]] = block.reshape(pairs, peer, block.shape[1])

    shared = len(HEADS_OF[0]) * HEAD_DIM
    for k, source in enumerate((key, value)):
        moved = by_tile(source)
        for lane in range(lanes):
            for tile in range(lanes):
                for j, h in enumerate(HEADS_OF[lane]):
                    put(lane, (2 * tile + k) * shared + j * HEAD_DIM, head(moved[tile], h))
    start = 2 * lanes * shared
    for name, source in zip(FIRST, others):
        place_rows(name, by_tile(source), put, start, lanes)
        start += width
    away = lax.rem(window[...] - me[0] + tiles, tiles)
    listed = jnp.where(away <= REACH, away + REACH, away - (tiles - REACH))
    missing = 5 * REACH - jnp.sum(listed, axis=1, keepdims=True)
    noted = jnp.broadcast_to(missing.astype(jnp.float32), (half, HEAD_DIM)).astype(jnp.bfloat16)
    for lane in range(lanes):
        put(lane, start, noted)


def add_up(parts):
    total = parts[0].astype(jnp.float32)
    for k in range(1, parts.shape[0]):
        total = total + parts[k].astype(jnp.float32)
    return total.astype(jnp.bfloat16)


def second_kernel(parts, order, *refs):
    *others, send = refs
    pairs, lanes, peer, _ = send.shape
    half = pairs * peer
    one_hot = order[...]

    def by_tile(product_of):
        moved = product_of.astype(jnp.bfloat16)
        return [moved[k * half : (k + 1) * half] for k in range(lanes)]

    def put(lane, start, block):
        send[:, lane, :, start : start + block.shape[1]] = block.reshape(pairs, peer, block.shape[1])

    start = 0
    for name, source in zip(SECOND, others):
        place_rows(name, by_tile(product(one_hot, source[...])), put, start, lanes)
        start += source.shape[1]
    low = jnp.concatenate(by_tile(product(one_hot, add_up(parts), NT)), axis=1)
    for lane in range(lanes):
        put(lane, start, low)


def unpack_kernel(received, after, key_value):
    tokens, width = key_value.shape[0] // 2, key_value.shape[1]
    for tile in range(2):
        key_value[tile * tokens : (tile + 1) * tokens, :] = received[:, :, tile * width : (tile + 1) * width].reshape(
            tokens, width
        )


def own_heads(up, own):
    return [jnp.where(own, head(up, a), head(up, b)) for a, b in zip(*HEADS_OF)]


def attend_kernel(me, left, right, centre, first, second, up, out, low_parts, up_part):
    tokens, width = out.shape
    rank = up.shape[0]
    lane = lax.rem(me[0], 2)
    own = lane == 0
    low_start = second.shape[2] - 2 * rank
    low = second[:, :, low_start : low_start + 2 * rank].reshape(tokens, 2 * rank)
    noted = [first[pl.ds(me[0] - lane + tile, 1), :, first.shape[2] - HEAD_DIM :] for tile in range(2)]
    missing = [jnp.max(note.astype(jnp.float32)).astype(jnp.int32) for note in noted]

    def unit_of(name, at):
        start = first.shape[2] - HEAD_DIM - (len(FIRST) - FIRST.index(name)) * width
        return first[:, :, start + at.start : start + at.stop].reshape(tokens, HEAD_DIM)

    span = [(array, tile) for array in (left, centre, right) for tile in range(2)]

    def block(index, columns):
        array, tile = span[index]
        return array[tile * tokens : (tile + 1) * tokens, columns]

    def chosen(tile, columns):
        if tile is None:
            skip = jnp.where(own, missing[0], missing[1])
            blocks = []
            for k in range(4):
                near = jnp.where(own, block(k, columns), block(k + 1, columns))
                far = jnp.where(own, block(k + 1, columns), block(k + 2, columns))
                blocks.append(jnp.where(skip <= k, far, near))
            return jnp.concatenate(blocks, axis=0)
        return jnp.concatenate(
            [
                jnp.where(missing[tile] <= k, block(tile + k + 1, columns), block(tile + k, columns))
                for k in range(4)
            ],
            axis=0,
        )

    scale = 1.0 / math.sqrt(HEAD_DIM)
    ups = own_heads(up, own)
    low_own = jnp.where(own, low[:, :rank], low[:, rank:])
    low_of = [jnp.zeros((rank, tokens), jnp.float32) for _ in range(2)]
    up_of = [jnp.zeros((rank, HEAD_DIM), jnp.float32) for _ in ups]
    shared = len(ups) * HEAD_DIM
    places = [slice(unit * HEAD_DIM, (unit + 1) * HEAD_DIM) for unit in range(len(UNITS))]
    keys = [chosen(tile, slice(j * HEAD_DIM, (j + 1) * HEAD_DIM)) for j, tile in UNITS]
    values = [chosen(tile, slice(shared + j * HEAD_DIM, shared + (j + 1) * HEAD_DIM)) for j, tile in UNITS]
    lows = [low_own if tile is None else low[:, tile * rank : (tile + 1) * rank] for _, tile in UNITS]
    queries = [
        (unit_of("base", at).astype(jnp.float32) + product(rows, ups[j])).astype(jnp.bfloat16)
        for at, rows, (j, _) in zip(places, lows, UNITS)
    ]
    scores = [product(query, k, NT) * scale for query, k in zip(queries, keys)]
    grad_weights = [product(unit_of("grad", at), v, NT) for at, v in zip(places, values)]
    weights, grad_scores = [], []
    for score, grad_weight in zip(scores, grad_weights):
        exps = jnp.exp(score - jnp.max(score, axis=-1, keepdims=True))
        weight = exps * (1.0 / jnp.sum(exps, axis=-1, keepdims=True))
        row_dot = jnp.sum(weight * grad_weight, axis=-1, keepdims=True)
        grad_scores.append((weight * (grad_weight - row_dot)).astype(jnp.bfloat16))
        weights.append(weight.astype(jnp.bfloat16))
    for at, weight, value in zip(places, weights, values):
        out[:, at] = product(weight, value).astype(jnp.bfloat16)
    grad_queries = [(product(g, k) * scale).astype(jnp.bfloat16) for g, k in zip(grad_scores, keys)]
    for (j, tile), rows, grad_query in zip(UNITS, lows, grad_queries):
        low_grad = product(ups[j], grad_query, NT)
        up_of[j] = up_of[j] + product(rows, grad_query, TN)
        if tile is None:
            low_of = [
                low_of[0] + jnp.where(own, low_grad, 0.0),
                low_of[1] + jnp.where(own, 0.0, low_grad),
            ]
        else:
            low_of[tile] = low_of[tile] + low_grad
    for tile in range(2):
        low_parts[tile] = low_of[tile]
    for h in range(up_part.shape[1] // HEAD_DIM):
        halves = [up_of[heads.index(h)] if h in heads else jnp.zeros_like(up_of[0]) for heads in HEADS_OF]
        up_part[:, h * HEAD_DIM : (h + 1) * HEAD_DIM] = jnp.where(own, halves[0], halves[1])


def chip_kernel(me, parts, send):
    lane = lax.rem(me[0], 2)
    total = parts[0, lane]
    for k in range(1, parts.shape[0]):
        total = total + parts[k, lane]
    for k in range(send.shape[0]):
        send[k] = total.astype(send.dtype)


def down_kernel(parts, second, out, up_part, send):
    tokens, width = out.shape
    peers, peer, _ = send.shape
    start = SECOND.index("hidden") * width
    down_part = product(add_up(parts), second[:, :, start : start + width].reshape(tokens, width))
    sums = jnp.concatenate([up_part[...], down_part], axis=0).astype(jnp.bfloat16)
    send[:, :, :width] = out[...].reshape(peers, peer, width)
    send[:, :, width:] = sums.reshape(peers, peer, width)


def sum_kernel(received, totals):
    peers, peer, width = totals.shape
    count = peers * peer
    rows = lax.broadcasted_iota(jnp.int32, (count, count), 0)
    cols = lax.broadcasted_iota(jnp.int32, (count, count), 1)
    same = jnp.where(lax.rem(rows, peer) == lax.rem(cols, peer), 1.0, 0.0).astype(jnp.bfloat16)
    total = product(same, received[:, :, width:].reshape(count, width))
    totals[...] = total.astype(totals.dtype).reshape(peers, peer, width)


def finish_kernel(order, received, totals, attended, up_total, down_total):
    rank = up_total.shape[0]
    tokens, width = attended.shape
    pairs, lanes, peer, _ = received.shape
    tiles = []
    for tile in range(lanes):
        blocks = []
        for h in range(width // HEAD_DIM):
            for lane, heads in enumerate(HEADS_OF):
                for unit, (j, at) in enumerate(UNITS):
                    if heads[j] == h and (lane if at is None else at) == tile:
                        columns = slice(unit * HEAD_DIM, (unit + 1) * HEAD_DIM)
                        blocks.append(received[:, lane, :, columns].reshape(pairs * peer, HEAD_DIM))
        tiles.append(jnp.concatenate(blocks, axis=1))
    attended[...] = product(order[...], jnp.concatenate(tiles, axis=0), TN).astype(jnp.bfloat16)
    sums = totals[...].reshape(2 * rank, width).astype(jnp.float32)
    up_total[...] = sums[:rank]
    down_total[...] = sums[rank:]


def local(
    hidden_in,
    query_base,
    key_base,
    value_base,
    grad_out,
    adapter_down,
    adapter_up,
    tile_slot,
    window_table,
):
    tokens, width = hidden_in.shape
    rank = adapter_up.shape[0]
    tiles = lax.axis_size(SEQ)
    lanes = lax.axis_size("lane")
    pairs = tiles // lanes
    group = lax.axis_size(TP)
    peer = tokens // tiles
    shared = len(HEADS_OF[0]) * HEAD_DIM
    bf16, f32 = jnp.bfloat16, jnp.float32
    shape = jax.ShapeDtypeStruct
    me = lax.axis_index(SEQ).astype(jnp.int32).reshape(1)

    columns = 4 * shared + len(FIRST) * width + HEAD_DIM
    named = {"base": query_base, "grad": grad_out, "hidden": hidden_in}
    order, send, low_part = call(
        functools.partial(start_kernel, tiles),
        [
            shape((tokens, tokens), bf16),
            shape((pairs, lanes, peer, columns), bf16),
            shape((rank, tokens), f32),
        ],
        (me,),
        (
            tile_slot.reshape(tiles, 1, tokens),
            window_table,
            key_base,
            value_base,
            hidden_in,
            adapter_down.T,
            *(named[name] for name in FIRST if name != "hidden"),
        ),
        [pl.BlockSpec((1, 1, tokens), lambda i, me: (me[0], 0, 0))] + [None] * (5 + len(FIRST) - ("hidden" in FIRST)),
        START_BYTES,
    )
    first = swap(send.reshape(tiles, peer, columns), SEQ)
    low_parts = lax.all_gather(jnp.sum(lax.all_gather(low_part, "core"), axis=0), "chip")
    second_width = len(SECOND) * width + 2 * rank
    second_send = call(
        second_kernel,
        shape((pairs, lanes, peer, second_width), bf16),
        (),
        (low_parts, order, *(named[name] for name in SECOND)),
    )
    centre = call(
        unpack_kernel,
        shape((2 * tokens, 2 * shared), bf16),
        (),
        (first, second_send),
        [pl.BlockSpec((tiles, peer, 4 * shared), lambda i, *_: (0, 0, 0)), pl.BlockSpec(memory_space=pl.ANY)],
    )
    left, right = shifted(centre, 1), shifted(centre, -1)
    second = swap(second_send.reshape(tiles, peer, second_width), SEQ)
    out_tile, low_grad_parts, up_part = call(
        attend_kernel,
        [shape((tokens, width), bf16), shape((lanes, rank, tokens), f32), shape((rank, width), f32)],
        (me,),
        (left, right, centre, first, second, adapter_up),
    )
    low_grad_parts = call(
        chip_kernel,
        shape((group // CORES, rank, tokens), bf16),
        (me,),
        (lax.all_gather(low_grad_parts, ("lane", "core")),),
    )
    low_grad_parts = swap(low_grad_parts, "chip")
    back_send = call(
        down_kernel,
        shape((tiles, peer, 2 * width), bf16),
        (),
        (low_grad_parts, second, out_tile, up_part),
    )
    back = swap(back_send, SEQ)
    totals = swap(call(sum_kernel, shape((tiles, peer, width), bf16), (), (back,)), SEQ)
    attended, up_total, down_total = call(
        finish_kernel,
        [shape((tokens, width), bf16)] + [shape((rank, width), f32)] * 2,
        (),
        (order, back.reshape(pairs, lanes, peer, 2 * width), totals),
    )
    return attended, down_total.T, up_total


def solution(mesh):
    tiles, group = mesh.devices.shape
    lanes = len(HEADS_OF)
    return jax.shard_map(
        local,
        mesh=Mesh(
            mesh.devices.reshape(tiles // lanes, lanes, group // CORES, CORES), ("pair", "lane", "chip", "core")
        ),
        in_specs=(
            P(SEQ, TP),
            P(SEQ, TP),
            P(SEQ, TP),
            P(SEQ, TP),
            P(SEQ, TP),
            P(TP, None),
            P(None, TP),
            P(),
            P(SEQ, None),
        ),
        out_specs=(P(SEQ, TP), P(TP, None), P(None, TP)),
        check_vma=False,
    )
```
